256 devices in a mesh: mem: 32 (over z, y), cell: 8 (over x, core).
Axes of the slice: x: 4, y: 4, z: 8, core: 2. Of those that a mesh axis runs over, the one named last changes fastest.
Arguments:
- anomaly: bfloat16 [3145728, 256], P(('mem', 'cell')), may hold values from -0.28515625 to 0.28515625
- innovation: float32 [3145728], P(('mem', 'cell')), may hold values from -6 to 6
- obs_weight: float32 [3145728], P(('mem', 'cell')), may hold values from 0.3 to 3
- valid_count: int32 [256], P(('mem', 'cell')), may hold values from 2048 to 12288, as said below
- background: bfloat16 [256, 1048576], P('mem', 'cell'), may hold values from -6 to 6
Outputs:
- analysis: bfloat16 [256, 1048576], P('mem', 'cell')
The draws below stay inside these ranges and needn't reach their ends.
Inputs may be any that keep to these rules, and one draw needn't show every extreme that they name: The first valid_count[i] of the 12288 row slots of device i hold cloud-free pixels; one device holds exactly 12288.
All inputs are finite; a program needn't handle non-finite values.
Results may differ from the reference program's by a relative error of at most 0.0074.
Values may be sent and summed in bfloat16 or wider, within the bound.
A program may use at most 64 MiB of HBM per device.

```python
import math
import jax
import jax.numpy as jnp
from jax import lax

K = 256
OBS_DEV = 4096
SHARDS = 256
CAP = 12288
ROWS = 3145728
STATE = 1048576


def draw_valid_count(key, part):
    key_one, key_two = jax.random.split(jax.random.fold_in(key, 17))
    counts = jax.random.randint(key_one, (SHARDS,), OBS_DEV // 2, 2 * OBS_DEV + 1)
    chosen = jax.random.randint(key_two, (), 0, SHARDS)
    return jnp.where(jnp.arange(SHARDS) == chosen, 3 * OBS_DEV, counts).astype(jnp.int32)


def draw_anomaly(key, part):
    keys = jax.random.split(jax.random.fold_in(key, 29), 4)
    fan_scale = float(OBS_DEV * SHARDS // 64) ** (-0.5)
    patterns = 16
    noise = jax.random.normal(keys[0], (ROWS, K), jnp.float32)
    amplitude = 1.0
    coefs = jax.random.normal(keys[1], (ROWS, patterns), jnp.float32)
    signs = jnp.where(jax.random.bernoulli(keys[2], 0.5, (patterns, K)), 0.25, -0.25).astype(jnp.float32)
    common = jnp.zeros((ROWS, K), jnp.float32)
    for pattern in range(patterns):
        common = common + coefs[:, pattern:pattern + 1] * signs[pattern:pattern + 1, :]
    norming = 1.0 / math.sqrt(1.0 + amplitude)
    value = (noise + common) * norming
    value = jnp.clip(value, -4.5, 4.5)
    targets = jax.random.permutation(keys[3], SHARDS) % (K // 8)
    row_target = targets[jnp.arange(ROWS) // CAP]
    column_block = jnp.arange(K) // 8
    boost = jnp.where(row_target[:, None] == column_block[None, :], 8.0, 1.0).astype(jnp.float32)
    return (value * boost * fan_scale).astype(jnp.bfloat16)


def block_levels(rng, extent, shards, low, high):
    def one(axis_at, shards_of):
        heights = jax.random.uniform(jax.random.fold_in(jax.random.fold_in(rng, 6), axis_at), (shards_of,), jnp.float32, low / len(shards), high / len(shards))
        return jnp.repeat(jnp.exp(heights), extent[axis_at] // shards_of).reshape((-1,) + (1,) * (len(extent) - axis_at - 1))

    level = one(*shards[0])
    for cut in shards[1:]:
        level = level * one(*cut)
    return level


def centred(own_key, shape, width, limit, shards=(), kind=jnp.bfloat16):
    gain = block_levels(own_key, shape, shards, -0.22, 0.18) if shards else 1.0
    array = jax.random.normal(own_key, shape, jnp.float32) * width * gain
    return jnp.minimum(jnp.maximum(array, -limit), limit).astype(kind)


def setup_inputs(seed: int = 0) -> dict:
    arg_keys = jax.random.split(jax.random.key(seed), 6)
    anomaly = draw_anomaly(jax.random.fold_in(arg_keys[5], 71), 0)
    innovation = centred(arg_keys[1], (ROWS,), 1.0, 6.0, ((0, 256),), jnp.float32)
    obs_weight = jnp.clip(jnp.exp(math.log(3.0) - 2.3025851 * jax.random.uniform(arg_keys[2], (ROWS,), jnp.float32) ** block_levels(arg_keys[2], (ROWS,), ((0, 256),), -0.2, 0.2)), 0.3, 3.0)
    valid_count = draw_valid_count(jax.random.fold_in(arg_keys[5], 71), 0)
    background = centred(arg_keys[4], (K, STATE), 1.0, 6.0, ((0, 32), (1, 8)))
    return {"anomaly": anomaly, "innovation": innovation, "obs_weight": obs_weight, "valid_count": valid_count, "background": background}


def reference(anomaly, innovation, obs_weight, valid_count, background):
    members = anomaly.shape[1]
    stacked = anomaly.reshape(SHARDS, CAP, members)
    innov_rows = innovation.reshape(SHARDS, CAP)
    weight_rows = obs_weight.reshape(SHARDS, CAP)
    positions = jnp.arange(CAP, dtype=jnp.int32)

    def accumulate(totals, pieces):
        block, misfit_raw, weight_raw, count = pieces
        live = (positions < count).astype(jnp.float32)
        row_factor = weight_raw * live
        scaled = (block.astype(jnp.float32) * row_factor[:, None]).astype(jnp.bfloat16)
        scaled = lax.optimization_barrier(scaled).astype(jnp.float32)
        misfit = (misfit_raw * row_factor).astype(jnp.bfloat16)
        misfit = lax.optimization_barrier(misfit).astype(jnp.float32)
        gram = totals[0] + jnp.dot(scaled.T, scaled, precision=lax.Precision.HIGHEST)
        pull = totals[1] + jnp.dot(misfit, scaled, precision=lax.Precision.HIGHEST)
        return ((gram, pull), None)
    start = (jnp.zeros((members, members), jnp.float32), jnp.zeros((members,), jnp.float32))
    (gram, pull), unused = lax.scan(accumulate, start, (stacked, innov_rows, weight_rows, valid_count))
    precision = gram + (members - 1.0) * jnp.eye(members, dtype=jnp.float32)
    factor = jnp.linalg.cholesky(precision)
    middle = lax.linalg.triangular_solve(factor, pull[:, None], left_side=True, lower=True)
    shift_w = lax.linalg.triangular_solve(factor, middle, left_side=True, lower=True, transpose_a=True)[:, 0]
    inverse_lower = lax.linalg.triangular_solve(factor, jnp.eye(members, dtype=jnp.float32), left_side=True, lower=True)
    transform = math.sqrt(members - 1.0) * inverse_lower.T
    weights = (transform + shift_w[:, None]).astype(jnp.bfloat16)
    weights_wide = lax.optimization_barrier(weights).astype(jnp.float32)
    blocks = background.reshape(members, SHARDS, -1).transpose(1, 0, 2)

    def update(block):
        wide = block.astype(jnp.float32)
        mean_state = lax.optimization_barrier(jnp.mean(wide, axis=0))
        spread_b = (wide - mean_state).astype(jnp.bfloat16)
        spread_b = lax.optimization_barrier(spread_b).astype(jnp.float32)
        fresh = mean_state + jnp.dot(weights_wide.T, spread_b, precision=lax.Precision.HIGHEST)
        return fresh.astype(jnp.bfloat16)
    analysis = lax.map(update, blocks).transpose(1, 0, 2).reshape(members, -1)
    return analysis
```

```python
import functools
import math

import jax
import jax.numpy as jnp
from jax import lax
from jax.experimental import pallas as pl
from jax.experimental.pallas import tpu as pltpu
from jax.sharding import PartitionSpec as P

MESH = pl.DeviceIdType.MESH
F32, BF16 = jnp.float32, jnp.bfloat16
EXACT = lax.Precision.HIGHEST
NT = (((1,), (1,)), ((), ()))

Z, Y, X, C = 8, 4, 4, 2
BLOCK, GROUP = 32, 8
CHUNK = 1024
WIDE = 512

TURNS = (
    [(0, 1), (0, 2), (0, 3)] + [(dz, dy) for dy in range(4) for dz in (1, 7)],
    [(2, 0), (6, 0), (2, 1), (6, 1), (2, 2), (6, 2)],
    [(2, 3), (6, 3), (4, 0), (4, 1)],
    [(4, 2), (4, 3), (3, 0), (5, 0)],
    [(3, 1), (5, 1), (3, 2), (5, 2), (3, 3), (5, 3)],
)
MEMBER_PEERS = [offset for turn in TURNS for offset in turn]
PLANE_PEERS = [(dy, dx, dc) for dy in range(Y) for dx in range(X) for dc in range(C)][1:]


def wrapped(base, extent):
    shifted = [base]
    for step in range(1, extent):
        shifted.append(jnp.where(base + step >= extent, base + (step - extent), base + step))
    return shifted


def small_factor(tile, size, group):
    lane = lax.broadcasted_iota(jnp.int32, (size, 128), 1)
    row = lax.broadcasted_iota(jnp.int32, (size, 128), 0)
    work = jnp.where(lane < size, tile, jnp.where(lane - size == row, 1.0, 0.0))

    def tall(piece):
        return jnp.concatenate([piece] * (size // 8), axis=0)

    for first in range(0, size, group):
        spots = range(first, first + group)
        cols = [jnp.broadcast_to(work[:, j : j + 1], (size, 128)) for j in spots]
        rows = [jnp.broadcast_to(work[j : j + 1, :], (8, 128)) for j in spots]
        cross = {
            (u, v): jnp.broadcast_to(cols[v][first + u : first + u + 1, :], (8, 128))
            for v in range(group)
            for u in range(v, group)
        }
        for t in range(group):
            inverse = 1.0 / cross[t, t]
            for u in range(t + 1, group):
                ratio = cross[u, t] * inverse
                rows[u] = rows[u] - ratio * rows[t]
                cols[u] = cols[u] - tall(ratio) * cols[t]
                for v in range(u, group):
                    cross[v, u] = cross[v, u] - ratio * cross[v, t]
            below = jnp.where(row > first + t, cols[t] * tall(inverse), 0.0)
            work = work - below * tall(rows[t])
    diagonal = jnp.sum(jnp.where(lane == row, work, 0.0), axis=1, keepdims=True)
    scale = lax.rsqrt(diagonal)
    scale = scale * (1.5 - 0.5 * diagonal * scale * scale)
    lower = pltpu.roll(work, 128 - size, 1) * scale
    return jnp.where(lane < size, lower, 0.0)


def invert_factor(mat_ref, size, group):
    order = mat_ref.shape[0]
    for first in range(0, order, size):
        last = first + size
        base = first // 128 * 128
        shift = first - base
        rows = mat_ref[first:last, :]
        tile = rows[:, base : base + 128]
        if shift:
            tile = pltpu.roll(tile, 128 - shift, 1)
        inverse = small_factor(tile, size, group)
        panel = jnp.dot(inverse[:, :size], rows, precision=EXACT, preferred_element_type=F32)
        placed = pltpu.roll(inverse, shift, 1) if shift else inverse
        blank = jnp.zeros_like(placed)
        placed = jnp.concatenate([placed if b == base else blank for b in range(0, order, 128)], axis=1)
        lane = lax.broadcasted_iota(jnp.int32, (size, order), 1)
        step = jnp.where((lane >= first) & (lane < last), placed, panel)
        mat_ref[first:last, :] = step
        if last < order:
            left = panel.T[last:, :]
            old = mat_ref[last:, :]
            lane = lax.broadcasted_iota(jnp.int32, old.shape, 1)
            old = jnp.where((lane >= first) & (lane < last), 0.0, old)
            mat_ref[last:, :] = old - jnp.dot(left, step, precision=EXACT, preferred_element_type=F32)


def kernel(
    count_ref, anom_ref, innov_ref, weight_ref, back_ref, out_ref,
    rows_v, innov_v, weight_v, gram_v, parts_v, layers_v, whole_v, mine_v, mat_v, block_v, fresh_v,
    in_sems, fwd_send, fwd_recv, bwd_send, bwd_recv, own_sems,
    plane_send, plane_recv, layer_send, layer_recv, all_send, all_recv,
):
    mem, cell = lax.axis_index("mem"), lax.axis_index("cell")
    z, y = lax.div(mem, Y), lax.rem(mem, Y)
    x, c = lax.div(cell, C), lax.rem(cell, C)
    zs, ys, xs, cs = wrapped(z, Z), wrapped(y, Y), wrapped(x, X), wrapped(c, C)
    capacity, members = rows_v.shape
    groups, local, width = block_v.shape
    chunks = capacity // CHUNK

    def member_dev(offset):
        return (zs[offset[0]] * Y + ys[offset[1]], cell)

    def plane_dev(offset):
        return (z * Y + ys[offset[0]], xs[offset[1]] * C + cs[offset[2]])

    def slot_of(offset):
        return ys[offset[0]] * (X * C) + xs[offset[1]] * C + cs[offset[2]]

    bring = [
        pltpu.make_async_copy(
            anom_ref.at[pl.ds(i * CHUNK, CHUNK), :], rows_v.at[pl.ds(i * CHUNK, CHUNK), :], in_sems.at[i]
        )
        for i in range(chunks)
    ]
    bring.append(pltpu.make_async_copy(innov_ref, innov_v, in_sems.at[chunks]))
    bring.append(pltpu.make_async_copy(weight_ref, weight_v, in_sems.at[chunks + 1]))
    for copy in bring:
        copy.start()

    barrier = pltpu.get_barrier_semaphore()
    for offset in MEMBER_PEERS:
        pl.semaphore_signal(barrier, inc=1, device_id=member_dev(offset), device_id_type=MESH)
    for offset in PLANE_PEERS:
        if offset[1:] != (0, 0):
            pl.semaphore_signal(barrier, inc=1, device_id=plane_dev(offset), device_id_type=MESH)
    pl.semaphore_wait(barrier, len(MEMBER_PEERS) + Y * X * C - Y)

    def block_of(group):
        return pl.ds(pl.multiple_of(group * width, width), width)

    own_in = pltpu.make_async_copy(back_ref.at[:, block_of(mem)], block_v.at[mem], own_sems.at[0])
    own_in.start()
    forward = []

    def send_turn(turn):
        for offset in TURNS[turn]:
            n = len(forward)
            target = member_dev(offset)
            copy = pltpu.make_async_remote_copy(
                src_ref=back_ref.at[:, block_of(target[0])], dst_ref=block_v.at[mem],
                send_sem=fwd_send.at[n], recv_sem=fwd_recv.at[n], device_id=target, device_id_type=MESH,
            )
            copy.start()
            forward.append(copy)

    send_turn(0)

    identity = jnp.where(
        lax.broadcasted_iota(jnp.int32, (members, members), 0)
        == lax.broadcasted_iota(jnp.int32, (members, members), 1),
        1.0, 0.0,
    ).astype(BF16)
    count = count_ref[0]
    bring[chunks].wait()
    bring[chunks + 1].wait()
    gram = jnp.zeros((members, members), F32)
    pull = jnp.zeros((16, members), F32)
    for i in range(chunks):
        bring[i].wait()
        here = pl.ds(i * CHUNK, CHUNK)
        position = i * CHUNK + lax.broadcasted_iota(jnp.int32, (1, CHUNK), 1)
        factor = jnp.where(position < count, weight_v[:, here], 0.0)
        misfit = (innov_v[:, here] * factor).astype(BF16)
        misfit = jnp.broadcast_to(misfit.astype(F32), (16, CHUNK)).astype(BF16)
        flat = lax.dot_general(identity, rows_v[here, :], NT, preferred_element_type=F32)
        scaled = (flat * factor).astype(BF16)
        gram = gram + lax.dot_general(scaled, scaled, NT, preferred_element_type=F32)
        pull = pull + lax.dot_general(misfit, scaled, NT, preferred_element_type=F32)
    row = lax.broadcasted_iota(jnp.int32, (members, members), 0)
    lane = lax.broadcasted_iota(jnp.int32, (members, members), 1)
    pull = pull[:1, :]
    gram = jnp.where((row == 0) & (lane > 0), pull, gram)
    gram = jnp.where((row == 1) & (lane == members - 1), pull[:, :1], gram)
    shards = Y * X * C
    gram_v[...] = gram.reshape(shards, members // shards, members)

    sent = []
    arriving = []
    mine = slot_of((0, 0, 0))
    for n, offset in enumerate(PLANE_PEERS):
        copy = pltpu.make_async_remote_copy(
            src_ref=gram_v.at[slot_of(offset)], dst_ref=parts_v.at[n],
            send_sem=plane_send.at[n], recv_sem=plane_recv.at[n], device_id=plane_dev(offset), device_id_type=MESH,
        )
        copy.start()
        arriving.append(copy)
        sent.append(copy)
    send_turn(1)
    total = gram_v[mine]
    for n, copy in enumerate(arriving):
        copy.wait_recv()
        total = total + parts_v[n]
    mine_v[...] = total
    layers_v[z] = total
    arriving = []
    for step in range(1, Z):
        copy = pltpu.make_async_remote_copy(
            src_ref=mine_v, dst_ref=layers_v.at[z],
            send_sem=layer_send.at[step], recv_sem=layer_recv.at[step],
            device_id=(zs[step] * Y + y, cell), device_id_type=MESH,
        )
        copy.start()
        arriving.append(copy)
        sent.append(copy)
    send_turn(2)
    for copy in arriving:
        copy.wait_recv()
    total = layers_v[0]
    for layer in range(1, Z):
        total = total + layers_v[layer]
    whole_v[mine] = total
    arriving = []
    for n, offset in enumerate(PLANE_PEERS):
        copy = pltpu.make_async_remote_copy(
            src_ref=whole_v.at[mine], dst_ref=whole_v.at[mine],
            send_sem=all_send.at[n], recv_sem=all_recv.at[n], device_id=plane_dev(offset), device_id_type=MESH,
        )
        copy.start()
        arriving.append(copy)
        sent.append(copy)
    send_turn(3)
    for copy in arriving:
        copy.wait_recv()
    send_turn(4)

    packed = whole_v[...].reshape(members, members)
    pull = jnp.where(lane[:1, :] == 0, packed[1:2, members - 1 :], packed[:1, :])
    picks = jnp.where(lax.broadcasted_iota(jnp.int32, (8, members), 1) == 0, 1.0, 0.0)
    column = lax.dot_general(picks, packed, NT, precision=EXACT, preferred_element_type=F32)[:1, :]
    picks = jnp.where(lax.broadcasted_iota(jnp.int32, (8, members), 1) == 1, 1.0, 0.0)
    second = lax.dot_general(picks, packed, NT, precision=EXACT, preferred_element_type=F32)[:1, :]
    precision = jnp.where(row == 0, column, packed)
    precision = jnp.where((row == 1) & (lane == members - 1), second, precision)
    mat_v[...] = precision + jnp.where(row == lane, members - 1.0, 0.0)
    invert_factor(mat_v, BLOCK, GROUP)
    lower = jnp.where(lane <= row, mat_v[...], 0.0)
    middle = lax.dot_general(pull, lower, NT, precision=EXACT, preferred_element_type=F32)
    shift_w = jnp.dot(middle, lower, precision=EXACT, preferred_element_type=F32)
    mixing = (math.sqrt(members - 1.0) * lower + shift_w).astype(BF16)

    own_in.wait()
    for copy in forward:
        copy.wait_recv()
    for copy in forward:
        copy.wait_send()

    for part in range(width // WIDE):
        here = pl.ds(part * WIDE, WIDE)
        values = block_v[:, :, here].astype(F32).reshape(members, WIDE)
        mean = jnp.sum(values, axis=0, keepdims=True) * (1.0 / members)
        spread = (values - mean).astype(BF16)
        fresh = mean + jnp.dot(mixing, spread, preferred_element_type=F32)
        fresh_v[:, :, here] = fresh.reshape(groups, local, WIDE).astype(BF16)

    own_out = pltpu.make_async_copy(fresh_v.at[mem], out_ref.at[:, block_of(mem)], own_sems.at[1])
    own_out.start()
    backward = []
    for n, offset in enumerate(MEMBER_PEERS):
        target = member_dev(offset)
        copy = pltpu.make_async_remote_copy(
            src_ref=fresh_v.at[target[0]], dst_ref=out_ref.at[:, block_of(mem)],
            send_sem=bwd_send.at[n], recv_sem=bwd_recv.at[n], device_id=target, device_id_type=MESH,
        )
        copy.start()
        backward.append(copy)
    own_out.wait()
    for copy in backward:
        copy.wait()
    for copy in sent:
        copy.wait_send()


def on_device(anomaly, innovation, obs_weight, valid_count, background):
    capacity, members = anomaly.shape
    local, cells = background.shape
    groups = lax.axis_size("mem")
    width = cells // groups
    shards = Y * X * C
    share = members // shards
    anywhere = pl.BlockSpec(memory_space=pl.ANY)
    dma = pltpu.SemaphoreType.DMA
    peers = len(MEMBER_PEERS)
    return pl.pallas_call(
        kernel,
        out_shape=jax.ShapeDtypeStruct(background.shape, background.dtype),
        in_specs=[pl.BlockSpec(memory_space=pltpu.SMEM)] + [anywhere] * 4,
        out_specs=anywhere,
        scratch_shapes=[
            pltpu.VMEM((capacity, members), BF16),
            pltpu.VMEM((1, capacity), F32),
            pltpu.VMEM((1, capacity), F32),
            pltpu.VMEM((shards, share, members), F32),
            pltpu.VMEM((shards - 1, share, members), F32),
            pltpu.VMEM((Z, share, members), F32),
            pltpu.VMEM((shards, share, members), F32),
            pltpu.VMEM((share, members), F32),
            pltpu.VMEM((members, members), F32),
            pltpu.VMEM((groups, local, width), BF16),
            pltpu.VMEM((groups, local, width), BF16),
            dma((capacity // CHUNK + 2,)),
            dma((peers,)),
            dma((peers,)),
            dma((peers,)),
            dma((peers,)),
            dma((2,)),
            dma((shards - 1,)),
            dma((shards - 1,)),
            dma((Z,)),
            dma((Z,)),
            dma((shards - 1,)),
            dma((shards - 1,)),
        ],
        compiler_params=pltpu.CompilerParams(
            collective_id=0, has_side_effects=True, vmem_limit_bytes=56 * 2**20
        ),
        name="analysis",
    )(
        valid_count,
        anomaly,
        innovation.reshape(1, capacity),
        obs_weight.reshape(1, capacity),
        background,
    )


def solution(mesh):
    rows = P(("mem", "cell"))
    slab = P("mem", "cell")
    return jax.shard_map(
        on_device,
        mesh=mesh,
        in_specs=(P(("mem", "cell"), None), rows, rows, rows, slab),
        out_specs=slab,
        check_vma=False,
    )
```

```python
import itertools
import math

import jax
import jax.numpy as jnp
from jax import lax
from jax.experimental import pallas as pl
from jax.experimental.pallas import tpu as pltpu
from jax.sharding import PartitionSpec as P

MESH = pl.DeviceIdType.MESH
F32, BF16 = jnp.float32, jnp.bfloat16
EXACT = lax.Precision.HIGHEST
NT = (((1,), (1,)), ((), ()))

Z, Y, X, C = 8, 4, 4, 2
BLOCK, GROUP = 64, 8
SPLIT = 2
CHUNK = 2048
WIDE = 512

ORDER = [(dz, dy) for dz in (4, 3, 5, 2, 6, 1, 7, 0) for dy in range(Y) if (dz, dy) != (0, 0)]
FORDER = [(dz, dy) for dys in ((0, 1), (2, 3)) for dz in (1, 7, 2, 6, 0, 4, 3, 5) for dy in dys if (dz, dy) != (0, 0)]
COUNTS = (12, 12, 8, 2, 2, 2, 8)
SCATTER = (("x", "c"), ("y",))
SIZES = {"z": Z, "y": Y, "x": X, "c": C}


def offsets(axes):
    found = []
    for steps in itertools.product(*[range(SIZES[axis]) for axis in axes]):
        if any(steps):
            found.append(dict(zip(axes, steps)))
    return found


def wrapped(base, extent):
    shifted = [base]
    for step in range(1, extent):
        shifted.append(jnp.where(base + step >= extent, base + (step - extent), base + step))
    return shifted


def small_factor(tile, size, group):
    lane = lax.broadcasted_iota(jnp.int32, (size, 128), 1)
    row = lax.broadcasted_iota(jnp.int32, (size, 128), 0)
    work = jnp.where(lane < size, tile, jnp.where(lane - size == row, 1.0, 0.0))

    def tall(piece):
        return jnp.concatenate([piece] * (size // 8), axis=0)

    for first in range(0, size, group):
        spots = range(first, first + group)
        cols = [jnp.broadcast_to(work[:, j : j + 1], (size, 128)) for j in spots]
        rows = [jnp.broadcast_to(work[j : j + 1, :], (8, 128)) for j in spots]
        cross = {
            (u, v): jnp.broadcast_to(cols[v][first + u : first + u + 1, :], (8, 128))
            for v in range(group)
            for u in range(v, group)
        }
        for t in range(group):
            inverse = 1.0 / cross[t, t]
            for u in range(t + 1, group):
                ratio = cross[u, t] * inverse
                rows[u] = rows[u] - ratio * rows[t]
                cols[u] = cols[u] - tall(ratio) * cols[t]
                for v in range(u, group):
                    cross[v, u] = cross[v, u] - ratio * cross[v, t]
            below = jnp.where(row > first + t, cols[t] * tall(inverse), 0.0)
            work = work - below * tall(rows[t])
    diagonal = jnp.sum(jnp.where(lane == row, work, 0.0), axis=1, keepdims=True)
    scale = lax.rsqrt(diagonal)
    scale = scale * (1.5 - 0.5 * diagonal * scale * scale)
    lower = pltpu.roll(work, 128 - size, 1) * scale
    return jnp.where(lane < size, lower, 0.0)


def invert_factor(mat_ref, size, group):
    order = mat_ref.shape[0]
    for first in range(0, order, size):
        last = first + size
        base = first // 128 * 128
        shift = first - base
        rows = mat_ref[first:last, :]
        tile = rows[:, base : base + 128]
        if shift:
            tile = pltpu.roll(tile, 128 - shift, 1)
        inverse = small_factor(tile, size, group)
        panel = jnp.dot(inverse[:, :size], rows, precision=EXACT, preferred_element_type=F32)
        placed = pltpu.roll(inverse, shift, 1) if shift else inverse
        blank = jnp.zeros_like(placed)
        placed = jnp.concatenate([placed if b == base else blank for b in range(0, order, 128)], axis=1)
        lane = lax.broadcasted_iota(jnp.int32, (size, order), 1)
        step = jnp.where((lane >= first) & (lane < last), placed, panel)
        mat_ref[first:last, :] = step
        if last < order:
            left = panel.T[last:, :]
            old = mat_ref[last:, :]
            lane = lax.broadcasted_iota(jnp.int32, old.shape, 1)
            old = jnp.where((lane >= first) & (lane < last), 0.0, old)
            mat_ref[last:, :] = old - jnp.dot(left, step, precision=EXACT, preferred_element_type=F32)


def kernel(
    count_ref, anom_ref, innov_ref, weight_ref, back_ref, out_ref,
    rows_v, scaled_v, misfit_v, innov_v, weight_v, gram_v, layers_v, mat_v, block_v, fresh_v,
    in_sems, fwd_send, fwd_recv, bwd_send, bwd_recv, own_sems, sum_send, sum_recv, *steps_v,
):
    mem, cell = lax.axis_index("mem"), lax.axis_index("cell")
    place = {
        "z": wrapped(lax.div(mem, Y), Z),
        "y": wrapped(lax.rem(mem, Y), Y),
        "x": wrapped(lax.div(cell, C), X),
        "c": wrapped(lax.rem(cell, C), C),
    }
    capacity, members = rows_v.shape
    groups, local, width = block_v.shape
    chunks = capacity // CHUNK
    z = place["z"][0]

    def device(offset):
        at = {axis: place[axis][offset.get(axis, 0)] for axis in "zyxc"}
        return (at["z"] * Y + at["y"], at["x"] * C + at["c"])

    def index(axes, offset):
        at = 0
        for axis in axes:
            at = at * SIZES[axis] + place[axis][offset.get(axis, 0)]
        return at

    def member_dev(offset):
        return device({"z": offset[0], "y": offset[1]})

    bring = [
        pltpu.make_async_copy(
            anom_ref.at[pl.ds(i * CHUNK, CHUNK), :], rows_v.at[pl.ds(i * CHUNK, CHUNK), :], in_sems.at[i]
        )
        for i in range(chunks)
    ]
    bring.append(pltpu.make_async_copy(innov_ref, innov_v, in_sems.at[chunks]))
    bring.append(pltpu.make_async_copy(weight_ref, weight_v, in_sems.at[chunks + 1]))
    for copy in bring:
        copy.start()

    barrier = pltpu.get_barrier_semaphore()
    greeted = [{"z": dz, "y": dy} for dz, dy in ORDER]
    for axes in SCATTER:
        for offset in offsets(axes):
            if not set(axes) <= {"z", "y"}:
                if any(offset.get(axis, 0) for axis in "xc"):
                    greeted.append(offset)
    for offset in greeted:
        pl.semaphore_signal(barrier, inc=1, device_id=device(offset), device_id_type=MESH)
    pl.semaphore_wait(barrier, len(greeted))

    narrow = width // SPLIT

    def cells_of(group, part):
        return pl.ds(pl.multiple_of(group * width + part * narrow, narrow), narrow)

    own_in = pltpu.make_async_copy(
        back_ref.at[:, pl.ds(pl.multiple_of(mem * width, width), width)], block_v.at[mem], own_sems.at[0]
    )
    own_in.start()
    waiting = [(part, offset) for part in range(SPLIT) for offset in FORDER]
    forward = []

    def pump(count):
        for part, offset in waiting[len(forward) : len(forward) + count]:
            n = len(forward)
            target = member_dev(offset)
            copy = pltpu.make_async_remote_copy(
                src_ref=back_ref.at[:, cells_of(target[0], part)],
                dst_ref=block_v.at[mem, :, pl.ds(part * narrow, narrow)],
                send_sem=fwd_send.at[n], recv_sem=fwd_recv.at[n], device_id=target, device_id_type=MESH,
            )
            copy.start()
            forward.append(copy)

    pump(COUNTS[0])

    identity = jnp.where(
        lax.broadcasted_iota(jnp.int32, (members, members), 0)
        == lax.broadcasted_iota(jnp.int32, (members, members), 1),
        1.0, 0.0,
    ).astype(BF16)
    count = count_ref[0]
    bring[chunks].wait()
    bring[chunks + 1].wait()
    for i in range(chunks):
        bring[i].wait()
        here = pl.ds(i * CHUNK, CHUNK)
        position = i * CHUNK + lax.broadcasted_iota(jnp.int32, (1, CHUNK), 1)
        factor = jnp.where(position < count, weight_v[:, here], 0.0)
        flat = lax.dot_general(identity, rows_v[here, :], NT, preferred_element_type=F32)
        scaled_v[:, here] = (flat * factor).astype(BF16)
        misfit = (innov_v[:, here] * factor).astype(BF16)
        misfit_v[:, here] = jnp.broadcast_to(misfit.astype(F32), (16, CHUNK)).astype(BF16)
        pump(COUNTS[1] * (i + 1) // chunks - COUNTS[1] * i // chunks)
    gram = lax.dot_general(scaled_v[...], scaled_v[...], NT, preferred_element_type=F32)
    pull = lax.dot_general(misfit_v[...], scaled_v[...], NT, preferred_element_type=F32)
    row = lax.broadcasted_iota(jnp.int32, (members, members), 0)
    lane = lax.broadcasted_iota(jnp.int32, (members, members), 1)
    pull = pull[:1, :]
    gram = jnp.where((row == 0) & (lane > 0), pull, gram)
    gram = jnp.where((row == 1) & (lane == members - 1), pull[:, :1], gram)
    gram_v[...] = gram.reshape(gram_v.shape)

    sent = []
    def send(source, target, offset):
        n = len(sent)
        copy = pltpu.make_async_remote_copy(
            src_ref=source, dst_ref=target, send_sem=sum_send.at[n], recv_sem=sum_recv.at[n],
            device_id=device(offset), device_id_type=MESH,
        )
        copy.start()
        sent.append(copy)
        return copy

    held, count, levels = gram_v, gram_v.shape[0], len(SCATTER)
    for level, axes in enumerate(SCATTER):
        landing, kept = steps_v[2 * level], steps_v[2 * level + 1]
        part = kept.shape[0]
        arriving = [
            send(held.at[pl.ds(index(axes, offset) * part, part)], landing.at[pl.ds(n * part, part)], offset)
            for n, offset in enumerate(offsets(axes))
        ]
        pump(COUNTS[2 + level])
        total = held[pl.ds(index(axes, {}) * part, part)]
        for n, copy in enumerate(arriving):
            copy.wait_recv()
            total = total + landing[n * part : (n + 1) * part]
        kept[...] = total
        held = kept
    layers_v[z] = held[0]
    arriving = [send(held.at[0], layers_v.at[z], {"z": step}) for step in range(1, Z)]
    pump(COUNTS[4])
    for copy in arriving:
        copy.wait_recv()
    total = layers_v[0]
    for layer in range(1, Z):
        total = total + layers_v[layer]
    held = None
    for level, axes in reversed(list(enumerate(SCATTER))):
        whole = steps_v[2 * levels + level]
        part = steps_v[2 * level + 1].shape[0]
        here = pl.ds(index(axes, {}) * part, part)
        whole[here] = total.reshape((part,) + total.shape[-2:]) if held is None else held[...]
        arriving = [send(whole.at[here], whole.at[here], offset) for offset in offsets(axes)]
        pump(COUNTS[6 - level])
        for copy in arriving:
            copy.wait_recv()
        held = whole
    pump(len(waiting))

    packed = held[...].reshape(members, members)
    pull = jnp.where(lane[:1, :] == 0, packed[1:2, members - 1 :], packed[:1, :])
    picks = jnp.where(lax.broadcasted_iota(jnp.int32, (8, members), 1) == 0, 1.0, 0.0)
    column = lax.dot_general(picks, packed, NT, precision=EXACT, preferred_element_type=F32)[:1, :]
    picks = jnp.where(lax.broadcasted_iota(jnp.int32, (8, members), 1) == 1, 1.0, 0.0)
    second = lax.dot_general(picks, packed, NT, precision=EXACT, preferred_element_type=F32)[:1, :]
    precision = jnp.where(row == 0, column, packed)
    precision = jnp.where((row == 1) & (lane == members - 1), second, precision)
    mat_v[...] = precision + jnp.where(row == lane, members - 1.0, 0.0)
    invert_factor(mat_v, BLOCK, GROUP)
    lower = jnp.where(lane <= row, mat_v[...], 0.0)
    middle = lax.dot_general(pull, lower, NT, precision=EXACT, preferred_element_type=F32)
    shift_w = jnp.dot(middle, lower, precision=EXACT, preferred_element_type=F32)
    mixing = (math.sqrt(members - 1.0) * lower + shift_w).astype(BF16)

    own_in.wait()
    own_out, backward = [], []
    for part in range(SPLIT):
        for copy in forward[part * len(FORDER) : (part + 1) * len(FORDER)]:
            copy.wait_recv()
        for start in range(part * narrow, (part + 1) * narrow, WIDE):
            here = pl.ds(start, WIDE)
            values = block_v[:, :, here].astype(F32).reshape(members, WIDE)
            mean = jnp.sum(values, axis=0, keepdims=True) * (1.0 / members)
            spread = (values - mean).astype(BF16)
            fresh = mean + jnp.dot(mixing, spread, preferred_element_type=F32)
            fresh_v[:, :, here] = fresh.reshape(groups, local, WIDE).astype(BF16)
        here = pl.ds(part * narrow, narrow)
        for offset in ORDER:
            n = len(backward)
            target = member_dev(offset)
            copy = pltpu.make_async_remote_copy(
                src_ref=fresh_v.at[target[0], :, here], dst_ref=out_ref.at[:, cells_of(mem, part)],
                send_sem=bwd_send.at[n], recv_sem=bwd_recv.at[n], device_id=target, device_id_type=MESH,
            )
            copy.start()
            backward.append(copy)
        copy = pltpu.make_async_copy(fresh_v.at[mem, :, here], out_ref.at[:, cells_of(mem, part)], own_sems.at[1 + part])
        copy.start()
        own_out.append(copy)
    for copy in forward:
        copy.wait_send()
    for copy in own_out:
        copy.wait()
    for copy in backward:
        copy.wait()
    for copy in sent:
        copy.wait_send()


def on_device(anomaly, innovation, obs_weight, valid_count, background):
    capacity, members = anomaly.shape
    local, cells = background.shape
    groups = lax.axis_size("mem")
    width = cells // groups
    anywhere = pl.BlockSpec(memory_space=pl.ANY)
    dma = pltpu.SemaphoreType.DMA
    peers = groups - 1
    shards = Y * X * C
    share = members // shards
    scatters, gathers, sends, count = [], [], Z - 1, shards
    for axes in SCATTER:
        size = math.prod(SIZES[axis] for axis in axes)
        part = count // size
        scatters.append(pltpu.VMEM(((size - 1) * part, share, members), F32))
        scatters.append(pltpu.VMEM((part, share, members), F32))
        gathers.append(pltpu.VMEM((count, share, members), F32))
        sends += 2 * (size - 1)
        count = part
    return pl.pallas_call(
        kernel,
        out_shape=pltpu.VMEM(background.shape, background.dtype),
        in_specs=[pl.BlockSpec(memory_space=pltpu.SMEM)] + [anywhere] * 4,
        out_specs=pl.BlockSpec(memory_space=pltpu.VMEM),
        scratch_shapes=[
            pltpu.VMEM((capacity, members), BF16),
            pltpu.VMEM((members, capacity), BF16),
            pltpu.VMEM((16, capacity), BF16),
            pltpu.VMEM((1, capacity), F32),
            pltpu.VMEM((1, capacity), F32),
            pltpu.VMEM((shards, share, members), F32),
            pltpu.VMEM((Z, share, members), F32),
            pltpu.VMEM((members, members), F32),
            pltpu.VMEM((groups, local, width), BF16),
            pltpu.VMEM((groups, local, width), BF16),
            dma((capacity // CHUNK + 2,)),
            dma((SPLIT * peers,)),
            dma((SPLIT * peers,)),
            dma((SPLIT * peers,)),
            dma((SPLIT * peers,)),
            dma((1 + SPLIT,)),
            dma((sends,)),
            dma((sends,)),
            *scatters,
            *gathers,
        ],
        compiler_params=pltpu.CompilerParams(
            collective_id=0, has_side_effects=True, vmem_limit_bytes=56 * 2**20
        ),
        name="analysis",
    )(
        valid_count,
        anomaly,
        innovation.reshape(1, capacity),
        obs_weight.reshape(1, capacity),
        background,
    )


def solution(mesh):
    rows = P(("mem", "cell"))
    slab = P("mem", "cell")
    return jax.shard_map(
        on_device,
        mesh=mesh,
        in_specs=(P(("mem", "cell"), None), rows, rows, rows, slab),
        out_specs=slab,
        check_vma=False,
    )
```

```python
import itertools
import math

import jax
import jax.numpy as jnp
from jax import lax
from jax.experimental import pallas as pl
from jax.experimental.pallas import tpu as pltpu
from jax.sharding import PartitionSpec as P

MESH = pl.DeviceIdType.MESH
F32, BF16 = jnp.float32, jnp.bfloat16
EXACT = lax.Precision.HIGHEST
NT = (((1,), (1,)), ((), ()))

Z, Y, X, C = 8, 4, 4, 2
BLOCK = 64
SPLIT = 2
CHUNK = 2048
WIDE = 512

ORDER = [(dz, dy) for dz in (4, 3, 5, 2, 6, 1, 7, 0) for dy in range(Y) if (dz, dy) != (0, 0)]
BOTH = [(dz, dy) for dy in (1, 3, 2) for dz in (1, 7, 2, 6, 4, 3, 5)]
ALONG_Z = [(dz, 0) for dz in (4, 3, 5, 2, 6, 1, 7)]
ALONG_Y = [(0, dy) for dy in range(1, Y)]
EARLY = 15


def turns(part):
    return [(part, offset) for offset in BOTH], [(part, offset) for offset in ALONG_Z], [(part, offset) for offset in ALONG_Y]


(BOTH_A, Z_A, Y_A), (BOTH_B, Z_B, Y_B) = turns(0), turns(1)
QUEUE = BOTH_A[:EARLY] + Z_A + BOTH_A[EARLY:] + Y_A + Y_B + Z_B + BOTH_B
COUNTS = (5, 4, 6, 7, 12, 7, 14, 99)
SCATTER = (("x", "c"), ("y",))
GATHER = (("x", "c"), ("y",))
SIZES = {"z": Z, "y": Y, "x": X, "c": C}


def offsets(axes):
    found = []
    for steps in itertools.product(*[range(SIZES[axis]) for axis in axes]):
        if any(steps):
            found.append(dict(zip(axes, steps)))
    return found


def wrapped(base, extent):
    shifted = [base]
    for step in range(1, extent):
        shifted.append(jnp.where(base + step >= extent, base + (step - extent), base + step))
    return shifted


def small_factor(tile, size):
    tiles = size // 8
    lane8 = lax.broadcasted_iota(jnp.int32, (8, 128), 1)
    row8 = lax.broadcasted_iota(jnp.int32, (8, 128), 0)
    work = []
    for g in range(tiles):
        piece = tile[8 * g : 8 * g + 8, :]
        work.append(jnp.where(lane8 < size, piece, jnp.where(lane8 - size == row8 + 8 * g, 1.0, 0.0)))
    for g in range(tiles):
        first = 8 * g
        cols = [[jnp.broadcast_to(work[k][:, j : j + 1], (8, 128)) for k in range(g, tiles)] for j in range(first, first + 8)]
        rows = [jnp.broadcast_to(work[g][j : j + 1, :], (8, 128)) for j in range(8)]
        cross = {(u, v): jnp.broadcast_to(cols[v][0][u : u + 1, :], (8, 128)) for v in range(8) for u in range(v, 8)}
        for t in range(0, 8, 2):
            s = t + 1
            a, b, c = cross[t, t], cross[s, t], cross[s, s]
            inv_a = 1.0 / a
            inv_d = a * (1.0 / (a * c - b * b))
            f = b * inv_a
            rows[s] = rows[s] - f * rows[t]
            cols[s] = [q - f * p for q, p in zip(cols[s], cols[t])]
            second = {u: cross[u, s] - f * cross[u, t] for u in range(t + 2, 8)}
            for u in range(t + 2, 8):
                ru, su = cross[u, t] * inv_a, second[u] * inv_d
                rows[u] = rows[u] - (ru * rows[t] + su * rows[s])
                cols[u] = [q - (ru * p + su * r) for q, p, r in zip(cols[u], cols[t], cols[s])]
                for v in range(u, 8):
                    cross[v, u] = cross[v, u] - (ru * cross[v, t] + su * second[v])
            one, two = rows[t] * inv_a, rows[s] * inv_d
            for k in range(g, tiles):
                p, r = cols[t][k - g], cols[s][k - g]
                if k == g:
                    p, r = jnp.where(row8 > t, p, 0.0), jnp.where(row8 > s, r, 0.0)
                work[k] = work[k] - (p * one + r * two)
    lower = []
    for g in range(tiles):
        diagonal = jnp.sum(jnp.where(lane8 == row8 + 8 * g, work[g], 0.0), axis=1, keepdims=True)
        scale = lax.rsqrt(diagonal)
        scale = scale * (1.5 - 0.5 * diagonal * scale * scale)
        lower.append(jnp.where(lane8 < size, pltpu.roll(work[g], 128 - size, 1) * scale, 0.0))
    return jnp.concatenate(lower, axis=0)


def invert_factor(mat_ref, size):
    order = mat_ref.shape[0]
    for first in range(0, order, size):
        last = first + size
        base = first // 128 * 128
        shift = first - base
        rows = mat_ref[first:last, :]
        tile = rows[:, base : base + 128]
        if shift:
            tile = pltpu.roll(tile, 128 - shift, 1)
        inverse = small_factor(tile, size)
        panel = jnp.dot(inverse[:, :size], rows, precision=EXACT, preferred_element_type=F32)
        placed = pltpu.roll(inverse, shift, 1) if shift else inverse
        blank = jnp.zeros_like(placed)
        placed = jnp.concatenate([placed if b == base else blank for b in range(0, order, 128)], axis=1)
        lane = lax.broadcasted_iota(jnp.int32, (size, order), 1)
        step = jnp.where((lane >= first) & (lane < last), placed, panel)
        mat_ref[first:last, :] = step
        if last < order:
            left = panel.T[last:, :]
            old = mat_ref[last:, :]
            lane = lax.broadcasted_iota(jnp.int32, old.shape, 1)
            old = jnp.where((lane >= first) & (lane < last), 0.0, old)
            mat_ref[last:, :] = old - jnp.dot(left, step, precision=EXACT, preferred_element_type=F32)


def kernel(
    count_ref, anom_ref, innov_ref, weight_ref, back_ref, out_ref,
    rows_v, scaled_v, misfit_v, innov_v, weight_v, gram_v, layers_v, mat_v, block_v, fresh_v,
    count_v, in_sems, fwd_send, fwd_recv, bwd_send, bwd_recv, own_sems, sum_send, sum_recv, *steps_v,
):
    mem, cell = lax.axis_index("mem"), lax.axis_index("cell")
    place = {
        "z": wrapped(lax.div(mem, Y), Z),
        "y": wrapped(lax.rem(mem, Y), Y),
        "x": wrapped(lax.div(cell, C), X),
        "c": wrapped(lax.rem(cell, C), C),
    }
    capacity, members = rows_v.shape
    groups, local, width = block_v.shape
    chunks = capacity // CHUNK
    z = place["z"][0]

    def device(offset):
        at = {axis: place[axis][offset.get(axis, 0)] for axis in "zyxc"}
        return (at["z"] * Y + at["y"], at["x"] * C + at["c"])

    def index(axes, offset):
        at = 0
        for axis in axes:
            at = at * SIZES[axis] + place[axis][offset.get(axis, 0)]
        return at

    def member_dev(offset):
        return device({"z": offset[0], "y": offset[1]})

    bring = [
        pltpu.make_async_copy(
            anom_ref.at[pl.ds(i * CHUNK, CHUNK), :], rows_v.at[pl.ds(i * CHUNK, CHUNK), :], in_sems.at[i]
        )
        for i in range(chunks)
    ]
    bring.append(pltpu.make_async_copy(innov_ref, innov_v, in_sems.at[chunks]))
    bring.append(pltpu.make_async_copy(weight_ref, weight_v, in_sems.at[chunks + 1]))
    bring.append(pltpu.make_async_copy(count_ref, count_v, in_sems.at[chunks + 2]))
    for copy in bring[chunks:] + bring[:chunks]:
        copy.start()

    barrier = pltpu.get_barrier_semaphore()
    greeted = [{"z": dz, "y": dy} for dz, dy in ORDER]
    for axes in SCATTER + GATHER:
        for offset in offsets(axes):
            offset = {axis: step for axis, step in offset.items() if step}
            if offset not in greeted and ("x" in offset or "c" in offset):
                greeted.append(offset)
    for offset in greeted:
        pl.semaphore_signal(barrier, inc=1, device_id=device(offset), device_id_type=MESH)
    pl.semaphore_wait(barrier, len(greeted))

    narrow = width // SPLIT

    def cells_of(group, part):
        return pl.ds(pl.multiple_of(group * width + part * narrow, narrow), narrow)

    own_in = pltpu.make_async_copy(
        back_ref.at[:, pl.ds(pl.multiple_of(mem * width, width), width)], block_v.at[mem], own_sems.at[0]
    )
    own_in.start()
    forward = []

    def pump(count):
        for part, offset in QUEUE[len(forward) : len(forward) + count]:
            n = len(forward)
            target = member_dev(offset)
            copy = pltpu.make_async_remote_copy(
                src_ref=back_ref.at[:, cells_of(target[0], part)],
                dst_ref=block_v.at[mem, :, pl.ds(part * narrow, narrow)],
                send_sem=fwd_send.at[n], recv_sem=fwd_recv.at[n], device_id=target, device_id_type=MESH,
            )
            copy.start()
            forward.append((part, copy))

    pump(COUNTS[0])

    identity = jnp.where(
        lax.broadcasted_iota(jnp.int32, (members, members), 0)
        == lax.broadcasted_iota(jnp.int32, (members, members), 1),
        1.0, 0.0,
    ).astype(BF16)
    for copy in bring[chunks:]:
        copy.wait()
    count = count_v[0]
    for i in range(chunks):
        bring[i].wait()
        here = pl.ds(i * CHUNK, CHUNK)
        position = i * CHUNK + lax.broadcasted_iota(jnp.int32, (1, CHUNK), 1)
        factor = jnp.where(position < count, weight_v[:, here], 0.0)
        flat = lax.dot_general(identity, rows_v[here, :], NT, preferred_element_type=F32)
        scaled_v[:, here] = (flat * factor).astype(BF16)
        misfit = (innov_v[:, here] * factor).astype(BF16)
        misfit_v[:, here] = jnp.broadcast_to(misfit.astype(F32), (16, CHUNK)).astype(BF16)
        pump(COUNTS[1] * (i + 1) // chunks - COUNTS[1] * i // chunks)
    gram = lax.dot_general(scaled_v[...], scaled_v[...], NT, preferred_element_type=F32)
    pull = lax.dot_general(misfit_v[...], scaled_v[...], NT, preferred_element_type=F32)
    row = lax.broadcasted_iota(jnp.int32, (members, members), 0)
    lane = lax.broadcasted_iota(jnp.int32, (members, members), 1)
    pull = pull[:1, :]
    gram = jnp.where((row == 0) & (lane > 0), pull, gram)
    gram = jnp.where((row == 1) & (lane == members - 1), pull[:, :1], gram)
    gram_v[...] = gram.reshape(gram_v.shape)

    sent = []
    def send(source, target, offset):
        n = len(sent)
        copy = pltpu.make_async_remote_copy(
            src_ref=source, dst_ref=target, send_sem=sum_send.at[n], recv_sem=sum_recv.at[n],
            device_id=device(offset), device_id_type=MESH,
        )
        copy.start()
        sent.append(copy)
        return copy

    held, count, levels = gram_v, gram_v.shape[0], len(SCATTER)
    for level, axes in enumerate(SCATTER):
        landing, kept = steps_v[2 * level], steps_v[2 * level + 1]
        part = kept.shape[0]
        arriving = [
            send(held.at[pl.ds(index(axes, offset) * part, part)], landing.at[pl.ds(n * part, part)], offset)
            for n, offset in enumerate(offsets(axes))
        ]
        pump(COUNTS[2 + level])
        total = held[pl.ds(index(axes, {}) * part, part)]
        for n, copy in enumerate(arriving):
            copy.wait_recv()
            total = total + landing[n * part : (n + 1) * part]
        kept[...] = total
        held = kept
    layers_v[z] = held[0]
    arriving = [send(held.at[0], layers_v.at[z], {"z": step}) for step in range(1, Z)]
    pump(COUNTS[4])
    for copy in arriving:
        copy.wait_recv()
    total = layers_v[0]
    for layer in range(1, Z):
        total = total + layers_v[layer]
    held = total.reshape((1,) + total.shape)
    for level, axes in reversed(list(enumerate(GATHER))):
        whole = steps_v[2 * levels + level]
        part = held.shape[0]
        here = pl.ds(index(axes, {}) * part, part)
        whole[here] = held[...]
        arriving = [send(whole.at[here], whole.at[here], offset) for offset in offsets(axes)]
        pump(COUNTS[6 - level])
        for copy in arriving:
            copy.wait_recv()
        held = whole
    pump(COUNTS[7])

    packed = held[...].reshape(members, members)
    pull = jnp.where(lane[:1, :] == 0, packed[1:2, members - 1 :], packed[:1, :])
    picks = jnp.where(lax.broadcasted_iota(jnp.int32, (8, members), 1) == 0, 1.0, 0.0)
    column = lax.dot_general(picks, packed, NT, precision=EXACT, preferred_element_type=F32)[:1, :]
    picks = jnp.where(lax.broadcasted_iota(jnp.int32, (8, members), 1) == 1, 1.0, 0.0)
    second = lax.dot_general(picks, packed, NT, precision=EXACT, preferred_element_type=F32)[:1, :]
    precision = jnp.where(row == 0, column, packed)
    precision = jnp.where((row == 1) & (lane == members - 1), second, precision)
    mat_v[...] = precision + jnp.where(row == lane, members - 1.0, 0.0)
    invert_factor(mat_v, BLOCK)
    lower = jnp.where(lane <= row, mat_v[...], 0.0)
    middle = lax.dot_general(pull, lower, NT, precision=EXACT, preferred_element_type=F32)
    shift_w = jnp.dot(middle, lower, precision=EXACT, preferred_element_type=F32)
    mixing = (math.sqrt(members - 1.0) * lower + shift_w).astype(BF16)

    own_in.wait()
    own_out, backward = [], []
    for part in range(SPLIT):
        for owner, copy in forward:
            if owner == part:
                copy.wait_recv()
        for start in range(part * narrow, (part + 1) * narrow, WIDE):
            here = pl.ds(start, WIDE)
            values = block_v[:, :, here].astype(F32).reshape(members, WIDE)
            mean = jnp.sum(values, axis=0, keepdims=True) * (1.0 / members)
            spread = (values - mean).astype(BF16)
            fresh = mean + jnp.dot(mixing, spread, preferred_element_type=F32)
            fresh_v[:, :, here] = fresh.reshape(groups, local, WIDE).astype(BF16)
        here = pl.ds(part * narrow, narrow)
        for offset in ORDER:
            n = len(backward)
            target = member_dev(offset)
            copy = pltpu.make_async_remote_copy(
                src_ref=fresh_v.at[target[0], :, here], dst_ref=out_ref.at[:, cells_of(mem, part)],
                send_sem=bwd_send.at[n], recv_sem=bwd_recv.at[n], device_id=target, device_id_type=MESH,
            )
            copy.start()
            backward.append(copy)
        copy = pltpu.make_async_copy(fresh_v.at[mem, :, here], out_ref.at[:, cells_of(mem, part)], own_sems.at[1 + part])
        copy.start()
        own_out.append(copy)
    for _, copy in forward:
        copy.wait_send()
    for copy in own_out:
        copy.wait()
    for copy in backward:
        copy.wait()
    for copy in sent:
        copy.wait_send()


def on_device(anomaly, innovation, obs_weight, valid_count, background):
    capacity, members = anomaly.shape
    local, cells = background.shape
    groups = lax.axis_size("mem")
    width = cells // groups
    anywhere = pl.BlockSpec(memory_space=pl.ANY)
    dma = pltpu.SemaphoreType.DMA
    peers = groups - 1
    shards = Y * X * C
    share = members // shards
    scatters, gathers, sends, count = [], [], Z - 1, shards
    for axes in SCATTER:
        size = math.prod(SIZES[axis] for axis in axes)
        part = count // size
        scatters.append(pltpu.VMEM(((size - 1) * part, share, members), F32))
        scatters.append(pltpu.VMEM((part, share, members), F32))
        sends += size - 1
        count = part
    count = shards
    for axes in GATHER:
        size = math.prod(SIZES[axis] for axis in axes)
        gathers.append(pltpu.VMEM((count, share, members), F32))
        sends += size - 1
        count //= size
    return pl.pallas_call(
        kernel,
        out_shape=pltpu.VMEM(background.shape, background.dtype),
        in_specs=[anywhere] * 5,
        out_specs=pl.BlockSpec(memory_space=pltpu.VMEM),
        scratch_shapes=[
            pltpu.VMEM((capacity, members), BF16),
            pltpu.VMEM((members, capacity), BF16),
            pltpu.VMEM((16, capacity), BF16),
            pltpu.VMEM((1, capacity), F32),
            pltpu.VMEM((1, capacity), F32),
            pltpu.VMEM((shards, share, members), F32),
            pltpu.VMEM((Z, share, members), F32),
            pltpu.VMEM((members, members), F32),
            pltpu.VMEM((groups, local, width), BF16),
            pltpu.VMEM((groups, local, width), BF16),
            pltpu.SMEM((1,), jnp.int32),
            dma((capacity // CHUNK + 3,)),
            dma((SPLIT * peers,)),
            dma((SPLIT * peers,)),
            dma((SPLIT * peers,)),
            dma((SPLIT * peers,)),
            dma((1 + SPLIT,)),
            dma((sends,)),
            dma((sends,)),
            *scatters,
            *gathers,
        ],
        compiler_params=pltpu.CompilerParams(
            collective_id=0, has_side_effects=True, vmem_limit_bytes=56 * 2**20
        ),
        name="analysis",
    )(
        valid_count,
        anomaly,
        innovation.reshape(1, capacity),
        obs_weight.reshape(1, capacity),
        background,
    )


def solution(mesh):
    rows = P(("mem", "cell"))
    slab = P("mem", "cell")
    return jax.shard_map(
        on_device,
        mesh=mesh,
        in_specs=(P(("mem", "cell"), None), rows, rows, rows, slab),
        out_specs=slab,
        check_vma=False,
    )
```

```python
import itertools
import math

import jax
import jax.numpy as jnp
from jax import lax
from jax.experimental import pallas as pl
from jax.experimental.pallas import tpu as pltpu
from jax.sharding import PartitionSpec as P

MESH = pl.DeviceIdType.MESH
F32, BF16 = jnp.float32, jnp.bfloat16
EXACT = lax.Precision.HIGHEST
NT = (((1,), (1,)), ((), ()))

Z, Y, X, C = 8, 4, 4, 2
BLOCK = 64
SPLIT = 2
CHUNK = 2048
WIDE = 512

ORDER = [(dz, dy) for dz in (0, 4, 3, 5, 2, 6, 1, 7) for dy in (2, 1, 3, 0) if (dz, dy) != (0, 0)]
BOTH = [(dz, dy) for dy in (1, 3, 2) for dz in (1, 7, 2, 6, 4, 3, 5)]
ALONG_Z = [(dz, 0) for dz in (4, 3, 5, 2, 6, 1, 7)]
ALONG_Y = [(0, dy) for dy in range(1, Y)]
EARLY = 15


def turns(part):
    return [(part, offset) for offset in BOTH], [(part, offset) for offset in ALONG_Z], [(part, offset) for offset in ALONG_Y]


(BOTH_A, Z_A, Y_A), (BOTH_B, Z_B, Y_B) = turns(0), turns(1)
QUEUE = BOTH_A[:EARLY] + Z_A + BOTH_A[EARLY:] + Y_A + Y_B + Z_B + BOTH_B
COUNTS = (5, 4, 6, 7, 12, 7, 14, 99)
SCATTER = (("x", "c"), ("y",))
GATHER = (("x", "c"), ("y",))
SIZES = {"z": Z, "y": Y, "x": X, "c": C}


def offsets(axes):
    found = []
    for steps in itertools.product(*[range(SIZES[axis]) for axis in axes]):
        if any(steps):
            found.append(dict(zip(axes, steps)))
    return found


def wrapped(base, extent):
    shifted = [base]
    for step in range(1, extent):
        shifted.append(jnp.where(base + step >= extent, base + (step - extent), base + step))
    return shifted


def small_factor(tile, size):
    tiles = size // 8
    lane8 = lax.broadcasted_iota(jnp.int32, (8, 128), 1)
    row8 = lax.broadcasted_iota(jnp.int32, (8, 128), 0)
    work = []
    for g in range(tiles):
        piece = tile[8 * g : 8 * g + 8, :]
        work.append(jnp.where(lane8 < size, piece, jnp.where(lane8 - size == row8 + 8 * g, 1.0, 0.0)))
    for g in range(tiles):
        first = 8 * g
        cols = [[jnp.broadcast_to(work[k][:, j : j + 1], (8, 128)) for k in range(g, tiles)] for j in range(first, first + 8)]
        rows = [jnp.broadcast_to(work[g][j : j + 1, :], (8, 128)) for j in range(8)]
        cross = {(u, v): jnp.broadcast_to(cols[v][0][u : u + 1, :], (8, 128)) for v in range(8) for u in range(v, 8)}
        for t in range(0, 8, 2):
            s = t + 1
            a, b, c = cross[t, t], cross[s, t], cross[s, s]
            inv_a = 1.0 / a
            inv_d = a * (1.0 / (a * c - b * b))
            f = b * inv_a
            rows[s] = rows[s] - f * rows[t]
            cols[s] = [q - f * p for q, p in zip(cols[s], cols[t])]
            second = {u: cross[u, s] - f * cross[u, t] for u in range(t + 2, 8)}
            for u in range(t + 2, 8):
                ru, su = cross[u, t] * inv_a, second[u] * inv_d
                rows[u] = rows[u] - (ru * rows[t] + su * rows[s])
                cols[u] = [q - (ru * p + su * r) for q, p, r in zip(cols[u], cols[t], cols[s])]
                for v in range(u, 8):
                    cross[v, u] = cross[v, u] - (ru * cross[v, t] + su * second[v])
            one, two = rows[t] * inv_a, rows[s] * inv_d
            for k in range(g, tiles):
                p, r = cols[t][k - g], cols[s][k - g]
                if k == g:
                    p, r = jnp.where(row8 > t, p, 0.0), jnp.where(row8 > s, r, 0.0)
                work[k] = work[k] - (p * one + r * two)
    lower = []
    for g in range(tiles):
        diagonal = jnp.sum(jnp.where(lane8 == row8 + 8 * g, work[g], 0.0), axis=1, keepdims=True)
        scale = lax.rsqrt(diagonal)
        scale = scale * (1.5 - 0.5 * diagonal * scale * scale)
        lower.append(jnp.where(lane8 < size, pltpu.roll(work[g], 128 - size, 1) * scale, 0.0))
    return jnp.concatenate(lower, axis=0)


def invert_factor(mat_ref, size):
    order = mat_ref.shape[0]
    for first in range(0, order, size):
        last = first + size
        base = first // 128 * 128
        shift = first - base
        rows = mat_ref[first:last, :]
        tile = rows[:, base : base + 128]
        if shift:
            tile = pltpu.roll(tile, 128 - shift, 1)
        inverse = small_factor(tile, size)
        panel = jnp.dot(inverse[:, :size], rows, precision=EXACT, preferred_element_type=F32)
        placed = pltpu.roll(inverse, shift, 1) if shift else inverse
        blank = jnp.zeros_like(placed)
        placed = jnp.concatenate([placed if b == base else blank for b in range(0, order, 128)], axis=1)
        lane = lax.broadcasted_iota(jnp.int32, (size, order), 1)
        step = jnp.where((lane >= first) & (lane < last), placed, panel)
        mat_ref[first:last, :] = step
        if last < order:
            left = panel.T[last:, :]
            old = mat_ref[last:, :]
            lane = lax.broadcasted_iota(jnp.int32, old.shape, 1)
            old = jnp.where((lane >= first) & (lane < last), 0.0, old)
            mat_ref[last:, :] = old - jnp.dot(left, step, precision=EXACT, preferred_element_type=F32)


def kernel(
    count_ref, anom_ref, innov_ref, weight_ref, back_ref, out_ref,
    rows_v, scaled_v, misfit_v, innov_v, weight_v, gram_v, layers_v, mat_v, block_v, fresh_v,
    count_v, in_sems, fwd_send, fwd_recv, bwd_send, bwd_recv, own_sems, sum_send, sum_recv, *steps_v,
):
    mem, cell = lax.axis_index("mem"), lax.axis_index("cell")
    place = {
        "z": wrapped(lax.div(mem, Y), Z),
        "y": wrapped(lax.rem(mem, Y), Y),
        "x": wrapped(lax.div(cell, C), X),
        "c": wrapped(lax.rem(cell, C), C),
    }
    capacity, members = rows_v.shape
    groups, local, width = block_v.shape
    chunks = capacity // CHUNK
    z = place["z"][0]

    def device(offset):
        at = {axis: place[axis][offset.get(axis, 0)] for axis in "zyxc"}
        return (at["z"] * Y + at["y"], at["x"] * C + at["c"])

    def index(axes, offset):
        at = 0
        for axis in axes:
            at = at * SIZES[axis] + place[axis][offset.get(axis, 0)]
        return at

    def member_dev(offset):
        return device({"z": offset[0], "y": offset[1]})

    bring = [
        pltpu.make_async_copy(
            anom_ref.at[pl.ds(i * CHUNK, CHUNK), :], rows_v.at[pl.ds(i * CHUNK, CHUNK), :], in_sems.at[i]
        )
        for i in range(chunks)
    ]
    bring.append(pltpu.make_async_copy(innov_ref, innov_v, in_sems.at[chunks]))
    bring.append(pltpu.make_async_copy(weight_ref, weight_v, in_sems.at[chunks + 1]))
    bring.append(pltpu.make_async_copy(count_ref, count_v, in_sems.at[chunks + 2]))

    barrier = pltpu.get_barrier_semaphore()
    greeted = [{"z": dz, "y": dy} for dz, dy in ORDER]
    for axes in SCATTER + GATHER:
        for offset in offsets(axes):
            offset = {axis: step for axis, step in offset.items() if step}
            if offset not in greeted and ("x" in offset or "c" in offset):
                greeted.append(offset)
    for offset in greeted:
        pl.semaphore_signal(barrier, inc=1, device_id=device(offset), device_id_type=MESH)
    for copy in bring[chunks:] + bring[:chunks]:
        copy.start()
    pl.semaphore_wait(barrier, len(greeted))

    narrow = width // SPLIT

    def cells_of(group, part):
        return pl.ds(pl.multiple_of(group * width + part * narrow, narrow), narrow)

    own_in = pltpu.make_async_copy(
        back_ref.at[:, pl.ds(pl.multiple_of(mem * width, width), width)], block_v.at[mem], own_sems.at[0]
    )
    own_in.start()
    forward = []

    def pump(count):
        for part, offset in QUEUE[len(forward) : len(forward) + count]:
            n = len(forward)
            target = member_dev(offset)
            copy = pltpu.make_async_remote_copy(
                src_ref=back_ref.at[:, cells_of(target[0], part)],
                dst_ref=block_v.at[mem, :, pl.ds(part * narrow, narrow)],
                send_sem=fwd_send.at[n], recv_sem=fwd_recv.at[n], device_id=target, device_id_type=MESH,
            )
            copy.start()
            forward.append((part, copy))

    pump(COUNTS[0])

    identity = jnp.where(
        lax.broadcasted_iota(jnp.int32, (members, members), 0)
        == lax.broadcasted_iota(jnp.int32, (members, members), 1),
        1.0, 0.0,
    ).astype(BF16)
    for copy in bring[chunks:]:
        copy.wait()
    count = count_v[0]
    for i in range(chunks):
        bring[i].wait()
        here = pl.ds(i * CHUNK, CHUNK)
        position = i * CHUNK + lax.broadcasted_iota(jnp.int32, (1, CHUNK), 1)
        factor = jnp.where(position < count, weight_v[:, here], 0.0)
        flat = lax.dot_general(identity, rows_v[here, :], NT, preferred_element_type=F32)
        scaled_v[:, here] = (flat * factor).astype(BF16)
        misfit = (innov_v[:, here] * factor).astype(BF16)
        misfit_v[:, here] = jnp.broadcast_to(misfit.astype(F32), (16, CHUNK)).astype(BF16)
        pump(COUNTS[1] * (i + 1) // chunks - COUNTS[1] * i // chunks)
    gram = lax.dot_general(scaled_v[...], scaled_v[...], NT, preferred_element_type=F32)
    pull = lax.dot_general(misfit_v[...], scaled_v[...], NT, preferred_element_type=F32)
    row = lax.broadcasted_iota(jnp.int32, (members, members), 0)
    lane = lax.broadcasted_iota(jnp.int32, (members, members), 1)
    pull = pull[:1, :]
    gram = jnp.where((row == 0) & (lane > 0), pull, gram)
    gram = jnp.where((row == 1) & (lane == members - 1), pull[:, :1], gram)
    gram_v[...] = gram.reshape(gram_v.shape)

    sent = []
    def send(source, target, offset):
        n = len(sent)
        copy = pltpu.make_async_remote_copy(
            src_ref=source, dst_ref=target, send_sem=sum_send.at[n], recv_sem=sum_recv.at[n],
            device_id=device(offset), device_id_type=MESH,
        )
        copy.start()
        sent.append(copy)
        return copy

    held, count, levels = gram_v, gram_v.shape[0], len(SCATTER)
    for level, axes in enumerate(SCATTER):
        landing, kept = steps_v[2 * level], steps_v[2 * level + 1]
        part = kept.shape[0]
        arriving = [
            send(held.at[pl.ds(index(axes, offset) * part, part)], landing.at[pl.ds(n * part, part)], offset)
            for n, offset in enumerate(offsets(axes))
        ]
        pump(COUNTS[2 + level])
        total = held[pl.ds(index(axes, {}) * part, part)]
        for n, copy in enumerate(arriving):
            copy.wait_recv()
            total = total + landing[n * part : (n + 1) * part]
        kept[...] = total
        held = kept
    layers_v[z] = held[0]
    arriving = [send(held.at[0], layers_v.at[z], {"z": step}) for step in range(1, Z)]
    pump(COUNTS[4])
    for copy in arriving:
        copy.wait_recv()
    total = layers_v[0]
    for layer in range(1, Z):
        total = total + layers_v[layer]
    held = total.reshape((1,) + total.shape)
    for level, axes in reversed(list(enumerate(GATHER))):
        whole = steps_v[2 * levels + level]
        part = held.shape[0]
        here = pl.ds(index(axes, {}) * part, part)
        whole[here] = held[...]
        arriving = [send(whole.at[here], whole.at[here], offset) for offset in offsets(axes)]
        pump(COUNTS[6 - level])
        for copy in arriving:
            copy.wait_recv()
        held = whole
    pump(COUNTS[7])

    packed = held[...].reshape(members, members)
    pull = jnp.where(lane[:1, :] == 0, packed[1:2, members - 1 :], packed[:1, :])
    picks = jnp.where(row[:8, :] == lane[:8, :], 1.0, 0.0)
    columns = lax.dot_general(picks, packed, NT, precision=EXACT, preferred_element_type=F32)
    precision = jnp.where(row == 0, columns[:1, :], packed)
    precision = jnp.where((row == 1) & (lane == members - 1), columns[1:2, :], precision)
    mat_v[...] = precision + jnp.where(row == lane, members - 1.0, 0.0)
    invert_factor(mat_v, BLOCK)
    lower = jnp.where(lane <= row, mat_v[...], 0.0)
    middle = lax.dot_general(pull, lower, NT, precision=EXACT, preferred_element_type=F32)
    shift_w = jnp.dot(middle, lower, precision=EXACT, preferred_element_type=F32)
    mixing = (math.sqrt(members - 1.0) * lower + shift_w).astype(BF16)

    own_in.wait()
    own_out, backward = [], []
    for part in range(SPLIT):
        for owner, copy in forward:
            if owner == part:
                copy.wait_recv()
        for start in range(part * narrow, (part + 1) * narrow, WIDE):
            here = pl.ds(start, WIDE)
            values = block_v[:, :, here].astype(F32).reshape(members, WIDE)
            mean = jnp.sum(values, axis=0, keepdims=True) * (1.0 / members)
            spread = (values - mean).astype(BF16)
            fresh = mean + jnp.dot(mixing, spread, preferred_element_type=F32)
            fresh_v[:, :, here] = fresh.reshape(groups, local, WIDE).astype(BF16)
        here = pl.ds(part * narrow, narrow)
        for offset in ORDER:
            n = len(backward)
            target = member_dev(offset)
            copy = pltpu.make_async_remote_copy(
                src_ref=fresh_v.at[target[0], :, here], dst_ref=out_ref.at[:, cells_of(mem, part)],
                send_sem=bwd_send.at[n], recv_sem=bwd_recv.at[n], device_id=target, device_id_type=MESH,
            )
            copy.start()
            backward.append(copy)
        copy = pltpu.make_async_copy(fresh_v.at[mem, :, here], out_ref.at[:, cells_of(mem, part)], own_sems.at[1 + part])
        copy.start()
        own_out.append(copy)
    for copy in [copy for _, copy in forward] + sent:
        copy.wait_send()
    for copy in own_out:
        copy.wait()
    for copy in backward:
        copy.wait_send()
    for copy in backward:
        copy.wait_recv()


def on_device(anomaly, innovation, obs_weight, valid_count, background):
    capacity, members = anomaly.shape
    local, cells = background.shape
    groups = lax.axis_size("mem")
    width = cells // groups
    anywhere = pl.BlockSpec(memory_space=pl.ANY)
    dma = pltpu.SemaphoreType.DMA
    peers = groups - 1
    shards = Y * X * C
    share = members // shards
    scatters, gathers, sends, count = [], [], Z - 1, shards
    for axes in SCATTER:
        size = math.prod(SIZES[axis] for axis in axes)
        part = count // size
        scatters.append(pltpu.VMEM(((size - 1) * part, share, members), F32))
        scatters.append(pltpu.VMEM((part, share, members), F32))
        sends += size - 1
        count = part
    count = shards
    for axes in GATHER:
        size = math.prod(SIZES[axis] for axis in axes)
        gathers.append(pltpu.VMEM((count, share, members), F32))
        sends += size - 1
        count //= size
    return pl.pallas_call(
        kernel,
        out_shape=pltpu.VMEM(background.shape, background.dtype),
        in_specs=[anywhere] * 5,
        out_specs=pl.BlockSpec(memory_space=pltpu.VMEM),
        scratch_shapes=[
            pltpu.VMEM((capacity, members), BF16),
            pltpu.VMEM((members, capacity), BF16),
            pltpu.VMEM((16, capacity), BF16),
            pltpu.VMEM((1, capacity), F32),
            pltpu.VMEM((1, capacity), F32),
            pltpu.VMEM((shards, share, members), F32),
            pltpu.VMEM((Z, share, members), F32),
            pltpu.VMEM((members, members), F32),
            pltpu.VMEM((groups, local, width), BF16),
            pltpu.VMEM((groups, local, width), BF16),
            pltpu.SMEM((1,), jnp.int32),
            dma((capacity // CHUNK + 3,)),
            dma((SPLIT * peers,)),
            dma((SPLIT * peers,)),
            dma((SPLIT * peers,)),
            dma((SPLIT * peers,)),
            dma((1 + SPLIT,)),
            dma((sends,)),
            dma((sends,)),
            *scatters,
            *gathers,
        ],
        compiler_params=pltpu.CompilerParams(
            collective_id=0, has_side_effects=True, vmem_limit_bytes=56 * 2**20
        ),
        name="analysis",
    )(
        valid_count,
        anomaly,
        innovation.reshape(1, capacity),
        obs_weight.reshape(1, capacity),
        background,
    )


def solution(mesh):
    rows = P(("mem", "cell"))
    slab = P("mem", "cell")
    return jax.shard_map(
        on_device,
        mesh=mesh,
        in_specs=(P(("mem", "cell"), None), rows, rows, rows, slab),
        out_specs=slab,
        check_vma=False,
    )
```
